32 devices in a mesh: freq: 4 (over z), space: 8 (over y, x, core).
Axes of the slice: x: 2, y: 2, z: 4, core: 2. Of those that a mesh axis runs over, the one named last changes fastest.
Arguments:
- wavefields: float32 [2, 4, 2, 2048, 2048], P(None, 'freq', None, 'space'), may hold values from -6 to 6
- frequencies: float32 [4], P('freq'), may hold values from 1.5 to 4
- velocity: float32 [16, 2048, 2048], P('freq', 'space'), may hold values from 1 to 2
- slab_owner: int32 [1], replicated, may hold values from 0 to 15
- ref_velocity: float32 [1, 2], replicated, may hold values from 1 to 2
- ref_index: int32 [1, 128], replicated, may hold values from 0 to 1
Outputs:
- extrapolated: float32 [2, 4, 2, 2048, 2048], P(None, 'freq', None, 'space')
- image: float32 [1, 2048, 2048], P(None, 'space')
The draws below stay inside these ranges and needn't reach their ends.
All inputs are finite; a program needn't handle non-finite values.
Results may differ from the reference program's by a relative error of at most 0.0003.
Values sent between devices are 32-bit elements; how exact they have to be, the bound alone decides.
A program may use at most 128 MiB of HBM per device.

```python
import math
import jax
import jax.numpy as jnp
from jax import lax

NX = 2048
NY = 2048
DEPTHS = 1
NREF = 2
RB = 16
DZ = 4
NW = 4
SLABS = 16
BLOCKS = 128


def place_ends(values, key, smallest, largest):
    spot = [jax.random.randint(jax.random.fold_in(key, axis), (), 0, length) for axis, length in enumerate(values.shape)]
    longest = values.shape.index(max(values.shape))
    beside = spot[:longest] + [(spot[longest] + 1) % values.shape[longest]] + spot[longest + 1:]
    return values.at[tuple(spot)].set(smallest).at[tuple(beside)].set(largest)


def block_scale(rng, shape, pieces, low, high):
    def one(axis_at, blocks):
        draws = jax.random.uniform(jax.random.fold_in(jax.random.fold_in(rng, 6), axis_at), (blocks,), jnp.float32, low / len(pieces), high / len(pieces))
        return jnp.repeat(jnp.exp(draws), shape[axis_at] // blocks).reshape((-1,) + (1,) * (len(shape) - axis_at - 1))

    gain = one(*pieces[0])
    for cut in pieces[1:]:
        gain = gain * one(*cut)
    return gain


def normal_values(rng, shape, scale, limit, cuts=(), kind=jnp.bfloat16):
    values = scale * jax.random.normal(rng, shape, jnp.float32)
    if cuts:
        values = values * block_scale(rng, shape, cuts, -0.22, 0.18)
    return jnp.clip(values, -limit, limit).astype(kind)


def setup_inputs(seed: int = 0) -> dict:
    key_of = jax.random.split(jax.random.key(seed), 7)
    wavefields = normal_values(key_of[0], (2, NW, 2, NX, NY), 1.0, 6.0, ((1, 4), (3, 8)), jnp.float32)
    frequencies = jnp.clip(jnp.exp(math.log(4.0) - 0.98082925 * jax.random.uniform(key_of[1], (NW,), jnp.float32) ** block_scale(key_of[1], (NW,), ((0, 4),), -0.2, 0.2)), 1.5, 4.0)
    velocity = jnp.clip(1.0 + 1.0 * jax.random.uniform(key_of[2], (SLABS, NX, NY), jnp.float32) ** block_scale(key_of[2], (SLABS, NX, NY), ((0, 4), (1, 8)), -0.2, 0.2), 1.0, 2.0)
    slab_owner = jax.random.randint(key_of[3], (DEPTHS,), 0, SLABS).astype(jnp.int32)
    ref_velocity = jnp.clip(jax.random.uniform(key_of[4], (DEPTHS, NREF), jnp.float32, 1.0, 2.0), 1.0, 2.0)
    ref_index = place_ends(jax.random.randint(key_of[5], (DEPTHS, BLOCKS), 0, NREF), jax.random.fold_in(key_of[5], 1), 0, NREF - 1).astype(jnp.int32)
    return {"wavefields": wavefields, "frequencies": frequencies, "velocity": velocity, "slab_owner": slab_owner, "ref_velocity": ref_velocity, "ref_index": ref_index}


def wave_numbers(length):
    counter = jnp.arange(length, dtype=jnp.int32)
    signed = jnp.where(counter < length // 2, counter, counter - length)
    return 2.0 * jnp.pi / length * signed.astype(jnp.float32)

def reference(wavefields, frequencies, velocity, slab_owner, ref_velocity, ref_index):
    field_signs = jnp.array([-1.0, 1.0], dtype=jnp.float32)[:, None, None]
    squared = wave_numbers(NX)[:, None] ** 2 + wave_numbers(NY)[None, :] ** 2
    fields = jnp.moveaxis(wavefields, 1, 0)
    images = []
    for depth_step in range(DEPTHS):
        slab_speed = velocity[slab_owner[depth_step]]
        row_refs = jnp.repeat(ref_index[depth_step], RB)
        ref_rows = ref_velocity[depth_step][row_refs]

        def advance(packed):
            wave_now, omega_one = packed
            complex_wave = wave_now[:, 0] + 1j * wave_now[:, 1]
            spectrum = jnp.fft.fft2(complex_wave)
            chosen = jnp.zeros_like(complex_wave)
            for ref_slot in range(NREF):
                vertical = (omega_one / ref_velocity[depth_step, ref_slot]) ** 2 - squared
                vertical_root = jnp.sqrt(jnp.abs(vertical))
                shift_phase = jnp.where(vertical >= 0.0, jnp.exp(1j * field_signs * DZ * vertical_root), jnp.exp(-DZ * vertical_root) + 0j)
                returned = jnp.fft.ifft2(spectrum * shift_phase)
                chosen = jnp.where((row_refs == ref_slot)[None, :, None], returned, chosen)
            split_phase = field_signs * omega_one * DZ * (1.0 / slab_speed - 1.0 / ref_rows[:, None])
            chosen = chosen * jnp.exp(1j * split_phase)
            coupling = DZ * (slab_speed - ref_rows[:, None]) * ref_rows[:, None] / (16.0 * omega_one)
            padded = jnp.pad(chosen, ((0, 0), (1, 1), (1, 1)))
            laplace = padded[:, 2:, 1:-1] + padded[:, :-2, 1:-1] + padded[:, 1:-1, 2:] + padded[:, 1:-1, :-2] - 4.0 * chosen
            result = chosen + 1j * field_signs * coupling * laplace
            return jnp.stack([jnp.real(result), jnp.imag(result)], axis=1)
        fields = lax.map(advance, (fields, frequencies))
        images.append(lax.optimization_barrier(jnp.sum(fields[:, 0, 0] * fields[:, 1, 0] + fields[:, 0, 1] * fields[:, 1, 1], axis=0)))
    return (jnp.moveaxis(fields, 0, 1), jnp.stack(images, axis=0))
```

```python
import functools
import math

import jax
import jax.numpy as jnp
import ml_dtypes
import numpy as np
from jax import lax
from jax.experimental import pallas as pl
from jax.experimental.pallas import tpu as pltpu
from jax.sharding import PartitionSpec as P

DZ = 4
LANES = 128
GROUP = 8
LIMIT = 56 * 1024 * 1024


def short_transform(values, direction):
    count = len(values)
    if count == 1:
        return values
    even = short_transform(values[0::2], direction)
    odd = short_transform(values[1::2], direction)
    low, high = [], []
    for k in range(count // 2):
        er, ei = even[k]
        orr, oi = odd[k]
        if k == 0:
            tr, ti = orr, oi
        elif 4 * k == count:
            tr, ti = (oi, -orr) if direction < 0 else (-oi, orr)
        else:
            c = math.cos(2.0 * math.pi * k / count)
            s = direction * math.sin(2.0 * math.pi * k / count)
            tr, ti = orr * c - oi * s, orr * s + oi * c
        low.append((er + tr, ei + ti))
        high.append((er - tr, ei - ti))
    return low + high


def halves(matrix):
    upper = matrix.astype(np.float32).astype(ml_dtypes.bfloat16)
    lower = (matrix - upper.astype(np.float64)).astype(ml_dtypes.bfloat16)
    return np.stack([upper, lower])


def block_matrix(direction, factor, left):
    index = np.arange(LANES)
    angle = direction * 2.0 * np.pi / LANES * (index[:, None] * index[None, :] % LANES)
    c, s = np.cos(angle) * factor, np.sin(angle) * factor
    matrix = np.block([[c, -s], [s, c]])
    return halves(matrix if left else matrix.T)


def twiddles(outer, spread):
    length = outer * LANES
    product = np.arange(outer)[:, None] * np.arange(LANES)[None, :] % length
    angle = -2.0 * np.pi / length * product
    table = np.stack([np.cos(angle), np.sin(angle)], axis=1).astype(np.float32)
    if spread:
        return np.ascontiguousarray(np.broadcast_to(table[..., None], table.shape + (spread,)))
    return table[:, :, None, :]


def split(values):
    upper = values.astype(jnp.bfloat16)
    return upper, (values - upper.astype(jnp.float32)).astype(jnp.bfloat16)


def dot(a, b):
    return jnp.dot(a, b, preferred_element_type=jnp.float32)


def times_right(values, matrix):
    upper, lower = split(values)
    return dot(upper, matrix[0]) + (dot(lower, matrix[0]) + dot(upper, matrix[1]))


def times_left(matrix, values):
    upper, lower = split(values)
    return dot(matrix[0], upper) + (dot(matrix[0], lower) + dot(matrix[1], upper))


def turn(value, c, s):
    return value[0] * c - value[1] * s, value[0] * s + value[1] * c


def rows_kernel(outer, cols_n, fields, table, matrix, out, scratch):
    rows = fields.shape[3]

    def group(i, carry):
        at = pl.ds(pl.multiple_of(i * GROUP, GROUP), GROUP)
        values = [
            tuple(fields[0, 0, c, at, a * LANES : (a + 1) * LANES] for c in range(2))
            for a in range(outer)
        ]
        values = short_transform(values, -1.0)
        for k, value in enumerate(values):
            re, im = turn(value, table[k, 0], table[k, 1]) if k else value
            scratch[k, at, :LANES] = re
            scratch[k, at, LANES:] = im
        return carry

    lax.fori_loop(0, rows // GROUP, group, 0)
    width = min(cols_n, LANES)
    for k in range(outer):
        both = times_right(scratch[k], matrix)
        for q in range(LANES // width):
            column = k * LANES + q * width
            dest, off = column // cols_n, column % cols_n
            for c in range(2):
                begin = c * LANES + q * width
                out[dest, c, :, off : off + width] = both[:, begin : begin + width]


def forward_rows(wavefields, j, space, cols_n):
    rows_n, length = wavefields.shape[3:]
    outer = length // LANES
    rows = math.gcd(rows_n, 64)
    whole = lambda *shape: pl.BlockSpec(shape, lambda i: (0,) * len(shape))
    return pl.pallas_call(
        functools.partial(rows_kernel, outer, cols_n),
        grid=(rows_n // rows,),
        in_specs=[
            pl.BlockSpec((1, 1, 2, rows, length), lambda i: (j, 0, 0, i, 0)),
            whole(outer, 2, 1, LANES),
            whole(2, 256, 256),
        ],
        out_specs=pl.BlockSpec((space, 2, rows, cols_n), lambda i: (0, 0, i, 0)),
        out_shape=jax.ShapeDtypeStruct((space, 2, rows_n, cols_n), jnp.float32),
        scratch_shapes=[pltpu.VMEM((outer, rows, 2 * LANES), jnp.float32)],
        compiler_params=pltpu.CompilerParams(vmem_limit_bytes=LIMIT),
        cost_estimate=pl.CostEstimate(
            flops=rows_n * length * 6000, bytes_accessed=rows_n * length * 16, transcendentals=0
        ),
    )(wavefields, jnp.asarray(twiddles(outer, 0)), jnp.asarray(block_matrix(-1.0, 1.0, False)))


def middle_kernel(outer, sign, rows_n, chunks, per_ref, *refs):
    chosen, fields, phase, table, forward, inverse = refs[:6]
    outs = refs[6 : 6 + chunks]
    spectrum, returned = refs[6 + chunks :]
    ref_count = phase.shape[0]
    part = rows_n // chunks
    lanes = fields.shape[3]

    def place(a, i):
        if rows_n >= LANES:
            return a * LANES // rows_n, a * LANES % rows_n, i * GROUP
        per = LANES // rows_n
        return a * per + i * GROUP // rows_n, 0, lax.rem(i * GROUP, rows_n)

    def first(i, carry):
        at = pl.multiple_of(i * GROUP, GROUP)
        values = []
        for a in range(outer):
            src, base, shift = place(a, i)
            row = pl.ds(pl.multiple_of(base + shift, GROUP), GROUP)
            values.append(tuple(fields[src, c, row, :] for c in range(2)))
        values = short_transform(values, -1.0)
        for k, value in enumerate(values):
            row = pl.ds(at, GROUP)
            if k:
                value = turn(value, table[k, 0, row, :], table[k, 1, row, :])
            for c in range(2):
                spectrum[k, pl.ds(at + c * LANES, GROUP), :] = value[c]
        return carry

    lax.fori_loop(0, LANES // GROUP, first, 0)

    def second(k, carry):
        both = times_left(forward, spectrum[k])
        re, im = both[:LANES], both[LANES:]
        for r in range(ref_count):
            shifted = turn((re, im), phase[r, 0, k], sign * phase[r, 1, k])
            returned[r, k] = times_left(inverse, jnp.concatenate(shifted, axis=0))
        return carry

    lax.fori_loop(0, outer, second, 0)

    def third(i, carry):
        at = pl.multiple_of(i * GROUP, GROUP)
        row = pl.ds(at, GROUP)
        for r in range(ref_count):
            values = []
            for k in range(outer):
                value = tuple(returned[r, k, pl.ds(at + c * LANES, GROUP), :] for c in range(2))
                if k:
                    value = turn(value, table[k, 0, row, :], -table[k, 1, row, :])
                values.append(value)
            values = short_transform(values, 1.0)
            for a, value in enumerate(values):
                src, base, shift = place(a, i)
                out = outs[base // part]
                target = pl.ds(pl.multiple_of(base % part + shift, GROUP), GROUP)
                for c in range(2):
                    if r:
                        mine = chosen[(a * LANES + i * GROUP) // per_ref] == r
                        kept = jnp.where(mine, value[c], out[src, c, target, :])
                    else:
                        kept = value[c]
                    out[src, c, target, :] = kept
        return carry

    lax.fori_loop(0, LANES // GROUP, third, 0)
    space = fields.shape[0]

    def edges(d, carry):
        for h in range(chunks):
            for side in range(2):
                slot = part + 2 * h + side
                if side == 0:
                    from_h = h - 1 if h else chunks - 1
                    from_d = d if h else jnp.maximum(d - 1, 0)
                    row = part - 1
                else:
                    from_h = h + 1 if h + 1 < chunks else 0
                    from_d = d if h + 1 < chunks else jnp.minimum(d + 1, space - 1)
                    row = 0
                for c in range(2):
                    outs[0][d, c, slot : slot + 1, :] = outs[from_h][from_d, c, row : row + 1, :]
        for c in range(2):
            outs[0][d, c, part + 2 * chunks : part + GROUP, :] = jnp.zeros(
                (GROUP - 2 * chunks, lanes), jnp.float32
            )
        return carry

    lax.fori_loop(0, space, edges, 0)


def middle(spectrum, phase, chosen, sign, chunks):
    space, _, rows_n, cols_n = spectrum.shape
    ref_count = phase.shape[0]
    length = space * rows_n
    outer = length // LANES
    width = math.gcd(cols_n, LANES)
    part = rows_n // chunks
    heights = [part + GROUP * (h == 0) for h in range(chunks)]
    whole = lambda *shape: pl.BlockSpec(shape, lambda i: (0,) * len(shape))
    return pl.pallas_call(
        functools.partial(
            middle_kernel, outer, sign, rows_n, chunks, length // chosen.shape[0]
        ),
        grid=(cols_n // width,),
        in_specs=[
            pl.BlockSpec(memory_space=pltpu.SMEM),
            pl.BlockSpec((space, 2, rows_n, width), lambda i: (0, 0, 0, i)),
            pl.BlockSpec((ref_count, 2, outer, LANES, width), lambda i: (0, 0, 0, 0, i)),
            whole(outer, 2, LANES, width),
            whole(2, 256, 256),
            whole(2, 256, 256),
        ],
        out_specs=[
            pl.BlockSpec((space, 2, height, width), lambda i: (0, 0, 0, i)) for height in heights
        ],
        out_shape=[
            jax.ShapeDtypeStruct((space, 2, height, cols_n), jnp.float32) for height in heights
        ],
        scratch_shapes=[
            pltpu.VMEM((outer, 2 * LANES, width), jnp.float32),
            pltpu.VMEM((ref_count, outer, 2 * LANES, width), jnp.float32),
        ],
        compiler_params=pltpu.CompilerParams(vmem_limit_bytes=LIMIT),
        cost_estimate=pl.CostEstimate(
            flops=length * cols_n * 20000, bytes_accessed=length * cols_n * 32, transcendentals=0
        ),
    )(
        chosen,
        spectrum,
        phase,
        jnp.asarray(twiddles(outer, width)),
        jnp.asarray(block_matrix(-1.0, 1.0, True)),
        jnp.asarray(block_matrix(1.0, 1.0 / length, True)),
    )


def final_kernel(outer, chunk, aliased, part, *refs):
    source, receiver, edge0, edge1, shift, shift_edge, beta, table, inverse = refs[:9]
    out, image = refs[9 + aliased : 11 + aliased]
    lines, wave = refs[11 + aliased :]
    cols_n = source.shape[3]
    width = min(cols_n, LANES)
    length = outer * LANES

    for j, (main, edge) in enumerate(((source, edge0), (receiver, edge1))):
        sign = -1.0 if j == 0 else 1.0

        for k in range(outer):
            pieces = []
            for c in range(2):
                for q in range(LANES // width):
                    column = k * LANES + q * width
                    src, off = column // cols_n, column % cols_n
                    span = slice(off, off + width)
                    pieces.append(
                        jnp.concatenate([main[src, c, :part, span], edge[src, c, :, span]], axis=0)
                    )
            both = times_right(jnp.concatenate(pieces, axis=1), inverse)
            lines[k] = both

        def lines_of(at):
            row = pl.ds(at, GROUP)
            values = []
            for k in range(outer):
                value = (lines[k, row, :LANES], lines[k, row, LANES:])
                if k:
                    value = turn(value, table[k, 0], -table[k, 1])
                values.append(value)
            return short_transform(values, 1.0)

        def group(i, carry):
            at = pl.multiple_of(i * GROUP, GROUP)
            row = pl.ds(at, GROUP)
            values = lines_of(at)
            for a, value in enumerate(values):
                span = slice(a * LANES, (a + 1) * LANES)
                value = turn(value, shift[0, row, span], sign * shift[1, row, span])
                for c in range(2):
                    wave[j, c, pl.ds(at + GROUP, GROUP), span] = value[c]
            return carry

        lax.fori_loop(0, part // GROUP, group, 0)
        values = lines_of(part)
        for a, value in enumerate(values):
            span = slice(a * LANES, (a + 1) * LANES)
            value = turn(value, shift_edge[0, :, span], sign * shift_edge[1, :, span])
            for c in range(2):
                wave[j, c, GROUP - 1 : GROUP, span] = value[c][2 * chunk : 2 * chunk + 1]
                wave[j, c, part + GROUP : part + GROUP + 1, span] = value[c][
                    2 * chunk + 1 : 2 * chunk + 2
                ]

    lane = lax.broadcasted_iota(jnp.int32, (GROUP, length), 1)
    line = lax.broadcasted_iota(jnp.int32, (GROUP, length), 0)

    def stencil(i, carry):
        at = pl.multiple_of(i * GROUP, GROUP)
        row = pl.ds(at, GROUP)
        factor = beta[row, :]
        total = jnp.zeros((GROUP, length), jnp.float32)
        kept = []
        for j in range(2):
            sign = -1.0 if j == 0 else 1.0
            laplace, centre = [], []
            for c in range(2):
                now = wave[j, c, pl.ds(at + GROUP, GROUP), :]
                before = wave[j, c, row, :]
                after = wave[j, c, pl.ds(at + 2 * GROUP, GROUP), :]
                up = jnp.where(line == 0, pltpu.roll(before, 1, 0), pltpu.roll(now, 1, 0))
                down = jnp.where(
                    line == GROUP - 1,
                    pltpu.roll(after, GROUP - 1, 0),
                    pltpu.roll(now, GROUP - 1, 0),
                )
                left = jnp.where(lane == 0, 0.0, pltpu.roll(now, 1, 1))
                right = jnp.where(lane == length - 1, 0.0, pltpu.roll(now, length - 1, 1))
                laplace.append(down + up + right + left - 4.0 * now)
                centre.append(now)
            scaled = sign * factor
            re = centre[0] - scaled * laplace[1]
            im = centre[1] + scaled * laplace[0]
            out[j, 0, 0, row, :] = re
            out[j, 0, 1, row, :] = im
            kept.append((re, im))
        image[row, :] = kept[0][0] * kept[1][0] + kept[0][1] * kept[1][1]
        return carry

    lax.fori_loop(0, part // GROUP, stencil, 0)


def final(main, edge, shift, shift_edge, beta, chunk, chunks, earlier):
    space, _, _, cols_n = main[0].shape
    part = shift.shape[1] // chunks
    length = space * cols_n
    outer = length // LANES
    aliased = int(earlier is not None)
    whole = lambda *shape: pl.BlockSpec(shape, lambda i: (0,) * len(shape))
    edge_spec = pl.BlockSpec((space, 2, GROUP, cols_n), lambda i: (0, 0, part // GROUP, 0))
    main_spec = pl.BlockSpec((space, 2, part, cols_n), lambda i: (0, 0, 0, 0))
    return pl.pallas_call(
        functools.partial(final_kernel, outer, chunk, aliased, part),
        grid=(1,),
        in_specs=[
            main_spec,
            main_spec,
            edge_spec,
            edge_spec,
            pl.BlockSpec((2, part, length), lambda i: (0, chunk, 0)),
            whole(2, GROUP, length),
            pl.BlockSpec((part, length), lambda i: (chunk, 0)),
            whole(outer, 2, 1, LANES),
            whole(2, 256, 256),
        ]
        + [pl.BlockSpec(memory_space=pl.ANY)] * aliased,
        out_specs=[
            pl.BlockSpec((2, 1, 2, part, length), lambda i: (0, 0, 0, chunk, 0)),
            whole(part, length),
        ],
        out_shape=[
            jax.ShapeDtypeStruct((2, 1, 2, part * chunks, length), jnp.float32),
            jax.ShapeDtypeStruct((part, length), jnp.float32),
        ],
        scratch_shapes=[
            pltpu.VMEM((outer, part + GROUP, 2 * LANES), jnp.float32),
            pltpu.VMEM((2, 2, part + 2 * GROUP, length), jnp.float32),
        ],
        input_output_aliases={9: 0} if aliased else {},
        compiler_params=pltpu.CompilerParams(vmem_limit_bytes=LIMIT),
        cost_estimate=pl.CostEstimate(
            flops=part * length * 15000, bytes_accessed=part * length * 60, transcendentals=0
        ),
    )(
        main[0],
        main[1],
        edge[0],
        edge[1],
        shift,
        shift_edge,
        beta,
        jnp.asarray(twiddles(outer, 0)),
        jnp.asarray(block_matrix(1.0, 1.0 / length, False)),
        *([earlier] if aliased else []),
    )


def wave_values(positions, length):
    outer = length // LANES
    natural_order = positions // LANES + outer * (positions % LANES)
    signed = jnp.where(natural_order < length // 2, natural_order, natural_order - length)
    return 2.0 * math.pi / length * signed.astype(jnp.float32)


def per_device(wavefields, frequencies, velocity, slab_owner, ref_velocity, ref_index):
    rows_n, width_y = wavefields.shape[3:]
    space = lax.axis_size("space")
    me = lax.axis_index("space")
    width_x = rows_n * space
    cols_n = width_y // space
    slab_local = velocity.shape[0]
    ref_count = ref_velocity.shape[1]
    chunks = 2 if rows_n >= 2 * LANES else 1
    part = rows_n // chunks
    omega = frequencies[0]

    owner = slab_owner[0]
    stored = lax.dynamic_index_in_dim(velocity, owner % slab_local, 0, keepdims=False)
    stored = jnp.where(lax.axis_index("freq") == owner // slab_local, stored, 0.0)
    speed = lax.psum(stored, "freq")

    swap = lambda x: lax.all_to_all(x, "space", split_axis=0, concat_axis=0, tiled=True)
    spectra = [swap(forward_rows(wavefields, j, space, cols_n)) for j in range(2)]

    ky = wave_values(me * cols_n + jnp.arange(cols_n, dtype=jnp.int32), width_y)
    kx = wave_values(jnp.arange(width_x, dtype=jnp.int32), width_x)
    squared = kx[:, None] ** 2 + ky[None, :] ** 2
    vertical = (omega / ref_velocity[0][:, None, None]) ** 2 - squared[None]
    root = jnp.sqrt(jnp.abs(vertical))
    fits = vertical >= 0.0
    cosine = jnp.where(fits, jnp.cos(DZ * root), jnp.exp(-DZ * root))
    sine = jnp.where(fits, jnp.sin(DZ * root), 0.0)
    phase = jnp.stack([cosine, sine], axis=1).reshape(
        ref_count, 2, width_x // LANES, LANES, cols_n
    )

    count = space
    above = lax.ppermute(speed[-1:], "space", [(i, i + 1) for i in range(count - 1)])
    below = lax.ppermute(speed[:1], "space", [(i + 1, i) for i in range(count - 1)])
    edge_rows, edge_speed = [], []
    for h in range(chunks):
        for local, outside, kept in (
            (h * part - 1, h == 0, above),
            ((h + 1) * part, h == chunks - 1, below),
        ):
            edge_rows.append(local)
            edge_speed.append(kept if outside else speed[local : local + 1])
    while len(edge_rows) < GROUP:
        edge_rows.append(0)
        edge_speed.append(speed[:1])
    block_refs = ref_index[0]
    per_ref = width_x // block_refs.shape[0]

    def shifts(c, rows):
        inside = (rows >= 0) & (rows < width_x)
        cr = ref_velocity[0][block_refs[jnp.clip(rows, 0, width_x - 1) // per_ref]][:, None]
        safe = jnp.where(inside[:, None], c, 1.0)
        angle = omega * DZ * (1.0 / safe - 1.0 / cr)
        keep = inside[:, None].astype(jnp.float32)
        return jnp.stack([jnp.cos(angle) * keep, jnp.sin(angle) * keep]), cr

    start = me * rows_n
    shift, cr = shifts(speed, start + jnp.arange(rows_n, dtype=jnp.int32))
    beta = DZ * (speed - cr) * cr / (16.0 * omega)
    shift_edge, _ = shifts(
        jnp.concatenate(edge_speed, axis=0), start + jnp.array(edge_rows, dtype=jnp.int32)
    )

    moved = []
    for j in range(2):
        moved.append(middle(spectra[j], phase, block_refs, -1.0 if j == 0 else 1.0, chunks))
    back = [[swap(moved[j][h]) for j in range(2)] for h in range(chunks)]
    fields, images = None, []
    for h in range(chunks):
        fields, image = final(back[h], back[0], shift, shift_edge, beta, h, chunks, fields)
        images.append(lax.psum(image, "freq"))
    return fields, jnp.concatenate(images, axis=0)[None]


def solution(mesh):
    in_specs = (
        P(None, "freq", None, "space", None),
        P("freq"),
        P("freq", "space", None),
        P(),
        P(),
        P(),
    )
    out_specs = (P(None, "freq", None, "space", None), P(None, "space", None))
    return jax.shard_map(
        per_device, mesh=mesh, in_specs=in_specs, out_specs=out_specs, check_vma=False
    )
```

```python
import functools
import math

import jax
import jax.numpy as jnp
import ml_dtypes
import numpy as np
from jax import lax
from jax.experimental import pallas as pl
from jax.experimental.pallas import tpu as pltpu
from jax.sharding import PartitionSpec as P

DZ = 4
LANES = 128
GROUP = 8
LIMIT = 56 * 1024 * 1024


def short_transform(values, direction):
    count = len(values)
    if count == 1:
        return values
    even = short_transform(values[0::2], direction)
    odd = short_transform(values[1::2], direction)
    low, high = [], []
    for k in range(count // 2):
        er, ei = even[k]
        orr, oi = odd[k]
        if k == 0:
            tr, ti = orr, oi
        elif 4 * k == count:
            tr, ti = (oi, -orr) if direction < 0 else (-oi, orr)
        else:
            c = math.cos(2.0 * math.pi * k / count)
            s = direction * math.sin(2.0 * math.pi * k / count)
            tr, ti = orr * c - oi * s, orr * s + oi * c
        low.append((er + tr, ei + ti))
        high.append((er - tr, ei - ti))
    return low + high


def halves(matrix):
    upper = matrix.astype(np.float32).astype(ml_dtypes.bfloat16)
    lower = (matrix - upper.astype(np.float64)).astype(ml_dtypes.bfloat16)
    return np.stack([upper, lower])


def block_matrix(direction, factor, left):
    index = np.arange(LANES)
    angle = direction * 2.0 * np.pi / LANES * (index[:, None] * index[None, :] % LANES)
    c, s = np.cos(angle) * factor, np.sin(angle) * factor
    matrix = np.block([[c, -s], [s, c]])
    return halves(matrix if left else matrix.T)


def twiddles(outer, spread):
    length = outer * LANES
    product = np.arange(outer)[:, None] * np.arange(LANES)[None, :] % length
    angle = -2.0 * np.pi / length * product
    table = np.stack([np.cos(angle), np.sin(angle)], axis=1).astype(np.float32)
    if spread:
        return np.ascontiguousarray(np.broadcast_to(table[..., None], table.shape + (spread,)))
    return table[:, :, None, :]


def split(values):
    upper = values.astype(jnp.bfloat16)
    return upper, (values - upper.astype(jnp.float32)).astype(jnp.bfloat16)


def dot(a, b):
    return jnp.dot(a, b, preferred_element_type=jnp.float32)


def times_right(values, matrix):
    upper, lower = split(values)
    return dot(upper, matrix[0]) + (dot(lower, matrix[0]) + dot(upper, matrix[1]))


def times_left(matrix, values):
    upper, lower = split(values)
    return dot(matrix[0], upper) + (dot(matrix[0], lower) + dot(matrix[1], upper))


def turn(value, c, s):
    return value[0] * c - value[1] * s, value[0] * s + value[1] * c


def rows_kernel(outer, cols_n, fields, table, matrix, out, scratch):
    rows = fields.shape[3]

    def group(i, carry):
        at = pl.ds(pl.multiple_of(i * GROUP, GROUP), GROUP)
        values = [
            tuple(fields[0, 0, c, at, a * LANES : (a + 1) * LANES] for c in range(2))
            for a in range(outer)
        ]
        values = short_transform(values, -1.0)
        for k, value in enumerate(values):
            re, im = turn(value, table[k, 0], table[k, 1]) if k else value
            scratch[k, at, :LANES] = re
            scratch[k, at, LANES:] = im
        return carry

    lax.fori_loop(0, rows // GROUP, group, 0)
    width = min(cols_n, LANES)
    for k in range(outer):
        both = times_right(scratch[k], matrix)
        for q in range(LANES // width):
            column = k * LANES + q * width
            dest, off = column // cols_n, column % cols_n
            for c in range(2):
                begin = c * LANES + q * width
                out[dest, c, :, off : off + width] = both[:, begin : begin + width]


def forward_rows(wavefields, j, space, cols_n):
    rows_n, length = wavefields.shape[3:]
    outer = length // LANES
    rows = math.gcd(rows_n, 64)
    whole = lambda *shape: pl.BlockSpec(shape, lambda i: (0,) * len(shape))
    return pl.pallas_call(
        functools.partial(rows_kernel, outer, cols_n),
        grid=(rows_n // rows,),
        in_specs=[
            pl.BlockSpec((1, 1, 2, rows, length), lambda i: (j, 0, 0, i, 0)),
            whole(outer, 2, 1, LANES),
            whole(2, 256, 256),
        ],
        out_specs=pl.BlockSpec((space, 2, rows, cols_n), lambda i: (0, 0, i, 0)),
        out_shape=jax.ShapeDtypeStruct((space, 2, rows_n, cols_n), jnp.float32),
        scratch_shapes=[pltpu.VMEM((outer, rows, 2 * LANES), jnp.float32)],
        compiler_params=pltpu.CompilerParams(vmem_limit_bytes=LIMIT),
        cost_estimate=pl.CostEstimate(
            flops=rows_n * length * 6000, bytes_accessed=rows_n * length * 16, transcendentals=0
        ),
    )(wavefields, jnp.asarray(twiddles(outer, 0)), jnp.asarray(block_matrix(-1.0, 1.0, False)))


def middle_kernel(outer, sign, rows_n, chunks, per_ref, *refs):
    chosen, fields, phase, table, forward, inverse = refs[:6]
    outs = refs[6 : 6 + chunks]
    spectrum, returned = refs[6 + chunks :]
    ref_count = phase.shape[0]
    part = rows_n // chunks
    lanes = fields.shape[3]

    def place(a, i):
        if rows_n >= LANES:
            return a * LANES // rows_n, a * LANES % rows_n, i * GROUP
        per = LANES // rows_n
        return a * per + i * GROUP // rows_n, 0, lax.rem(i * GROUP, rows_n)

    def first(i, carry):
        at = pl.multiple_of(i * GROUP, GROUP)
        values = []
        for a in range(outer):
            src, base, shift = place(a, i)
            row = pl.ds(pl.multiple_of(base + shift, GROUP), GROUP)
            values.append(tuple(fields[src, c, row, :] for c in range(2)))
        values = short_transform(values, -1.0)
        for k, value in enumerate(values):
            row = pl.ds(at, GROUP)
            if k:
                value = turn(value, table[k, 0, row, :], table[k, 1, row, :])
            for c in range(2):
                spectrum[k, pl.ds(at + c * LANES, GROUP), :] = value[c]
        return carry

    lax.fori_loop(0, LANES // GROUP, first, 0)

    def second(k, carry):
        both = times_left(forward, spectrum[k])
        re, im = both[:LANES], both[LANES:]
        for r in range(ref_count):
            shifted = turn((re, im), phase[r, 0, k], sign * phase[r, 1, k])
            returned[r, k] = times_left(inverse, jnp.concatenate(shifted, axis=0))
        return carry

    lax.fori_loop(0, outer, second, 0)

    def third(i, carry):
        at = pl.multiple_of(i * GROUP, GROUP)
        row = pl.ds(at, GROUP)
        for r in range(ref_count):
            values = []
            for k in range(outer):
                value = tuple(returned[r, k, pl.ds(at + c * LANES, GROUP), :] for c in range(2))
                if k:
                    value = turn(value, table[k, 0, row, :], -table[k, 1, row, :])
                values.append(value)
            values = short_transform(values, 1.0)
            for a, value in enumerate(values):
                src, base, shift = place(a, i)
                out = outs[base // part]
                target = pl.ds(pl.multiple_of(base % part + shift, GROUP), GROUP)
                for c in range(2):
                    if r:
                        mine = chosen[(a * LANES + i * GROUP) // per_ref] == r
                        kept = jnp.where(mine, value[c], out[src, c, target, :])
                    else:
                        kept = value[c]
                    out[src, c, target, :] = kept
        return carry

    lax.fori_loop(0, LANES // GROUP, third, 0)
    space = fields.shape[0]

    def edges(d, carry):
        for h in range(chunks):
            for side in range(2):
                slot = part + 2 * h + side
                if side == 0:
                    from_h = h - 1 if h else chunks - 1
                    from_d = d if h else jnp.maximum(d - 1, 0)
                    row = part - 1
                else:
                    from_h = h + 1 if h + 1 < chunks else 0
                    from_d = d if h + 1 < chunks else jnp.minimum(d + 1, space - 1)
                    row = 0
                for c in range(2):
                    outs[0][d, c, slot : slot + 1, :] = outs[from_h][from_d, c, row : row + 1, :]
        for c in range(2):
            outs[0][d, c, part + 2 * chunks : part + GROUP, :] = jnp.zeros(
                (GROUP - 2 * chunks, lanes), jnp.float32
            )
        return carry

    lax.fori_loop(0, space, edges, 0)


def middle(spectrum, phase, chosen, sign, chunks):
    space, _, rows_n, cols_n = spectrum.shape
    ref_count = phase.shape[0]
    length = space * rows_n
    outer = length // LANES
    width = math.gcd(cols_n, LANES)
    part = rows_n // chunks
    heights = [part + GROUP * (h == 0) for h in range(chunks)]
    whole = lambda *shape: pl.BlockSpec(shape, lambda i: (0,) * len(shape))
    return pl.pallas_call(
        functools.partial(
            middle_kernel, outer, sign, rows_n, chunks, length // chosen.shape[0]
        ),
        grid=(cols_n // width,),
        in_specs=[
            pl.BlockSpec(memory_space=pltpu.SMEM),
            pl.BlockSpec((space, 2, rows_n, width), lambda i: (0, 0, 0, i)),
            pl.BlockSpec((ref_count, 2, outer, LANES, width), lambda i: (0, 0, 0, 0, i)),
            whole(outer, 2, LANES, width),
            whole(2, 256, 256),
            whole(2, 256, 256),
        ],
        out_specs=[
            pl.BlockSpec((space, 2, height, width), lambda i: (0, 0, 0, i)) for height in heights
        ],
        out_shape=[
            jax.ShapeDtypeStruct((space, 2, height, cols_n), jnp.float32) for height in heights
        ],
        scratch_shapes=[
            pltpu.VMEM((outer, 2 * LANES, width), jnp.float32),
            pltpu.VMEM((ref_count, outer, 2 * LANES, width), jnp.float32),
        ],
        compiler_params=pltpu.CompilerParams(vmem_limit_bytes=LIMIT),
        cost_estimate=pl.CostEstimate(
            flops=length * cols_n * 20000, bytes_accessed=length * cols_n * 32, transcendentals=0
        ),
    )(
        chosen,
        spectrum,
        phase,
        jnp.asarray(twiddles(outer, width)),
        jnp.asarray(block_matrix(-1.0, 1.0, True)),
        jnp.asarray(block_matrix(1.0, 1.0 / length, True)),
    )


def final_kernel(outer, chunk, aliased, part, *refs):
    source, receiver, edge0, edge1, shift, shift_edge, beta, table, inverse = refs[:9]
    out, image = refs[9 + aliased : 11 + aliased]
    lines, wave = refs[11 + aliased :]
    cols_n = source.shape[3]
    width = min(cols_n, LANES)
    length = outer * LANES

    for j, (main, edge) in enumerate(((source, edge0), (receiver, edge1))):
        sign = -1.0 if j == 0 else 1.0

        for k in range(outer):
            pieces = []
            for c in range(2):
                for q in range(LANES // width):
                    column = k * LANES + q * width
                    src, off = column // cols_n, column % cols_n
                    span = slice(off, off + width)
                    pieces.append(
                        jnp.concatenate([main[src, c, :part, span], edge[src, c, :, span]], axis=0)
                    )
            both = times_right(jnp.concatenate(pieces, axis=1), inverse)
            lines[k] = both

        def lines_of(at):
            row = pl.ds(at, GROUP)
            values = []
            for k in range(outer):
                value = (lines[k, row, :LANES], lines[k, row, LANES:])
                if k:
                    value = turn(value, table[k, 0], -table[k, 1])
                values.append(value)
            return short_transform(values, 1.0)

        def group(i, carry):
            at = pl.multiple_of(i * GROUP, GROUP)
            row = pl.ds(at, GROUP)
            values = lines_of(at)
            for a, value in enumerate(values):
                span = slice(a * LANES, (a + 1) * LANES)
                value = turn(value, shift[0, row, span], sign * shift[1, row, span])
                for c in range(2):
                    wave[j, c, pl.ds(at + GROUP, GROUP), span] = value[c]
            return carry

        lax.fori_loop(0, part // GROUP, group, 0)
        values = lines_of(part)
        for a, value in enumerate(values):
            span = slice(a * LANES, (a + 1) * LANES)
            value = turn(value, shift_edge[0, :, span], sign * shift_edge[1, :, span])
            for c in range(2):
                wave[j, c, GROUP - 1 : GROUP, span] = value[c][2 * chunk : 2 * chunk + 1]
                wave[j, c, part + GROUP : part + GROUP + 1, span] = value[c][
                    2 * chunk + 1 : 2 * chunk + 2
                ]

    lane = lax.broadcasted_iota(jnp.int32, (GROUP, length), 1)
    line = lax.broadcasted_iota(jnp.int32, (GROUP, length), 0)

    def stencil(i, carry):
        at = pl.multiple_of(i * GROUP, GROUP)
        row = pl.ds(at, GROUP)
        factor = beta[row, :]
        total = jnp.zeros((GROUP, length), jnp.float32)
        kept = []
        for j in range(2):
            sign = -1.0 if j == 0 else 1.0
            laplace, centre = [], []
            for c in range(2):
                now = wave[j, c, pl.ds(at + GROUP, GROUP), :]
                before = wave[j, c, row, :]
                after = wave[j, c, pl.ds(at + 2 * GROUP, GROUP), :]
                up = jnp.where(line == 0, pltpu.roll(before, 1, 0), pltpu.roll(now, 1, 0))
                down = jnp.where(
                    line == GROUP - 1,
                    pltpu.roll(after, GROUP - 1, 0),
                    pltpu.roll(now, GROUP - 1, 0),
                )
                left = jnp.where(lane == 0, 0.0, pltpu.roll(now, 1, 1))
                right = jnp.where(lane == length - 1, 0.0, pltpu.roll(now, length - 1, 1))
                laplace.append(down + up + right + left - 4.0 * now)
                centre.append(now)
            scaled = sign * factor
            re = centre[0] - scaled * laplace[1]
            im = centre[1] + scaled * laplace[0]
            out[j, 0, 0, row, :] = re
            out[j, 0, 1, row, :] = im
            kept.append((re, im))
        image[row, :] = kept[0][0] * kept[1][0] + kept[0][1] * kept[1][1]
        return carry

    lax.fori_loop(0, part // GROUP, stencil, 0)


def final(main, edge, shift, shift_edge, beta, chunk, chunks, earlier):
    space, _, _, cols_n = main[0].shape
    part = shift.shape[1] // chunks
    length = space * cols_n
    outer = length // LANES
    aliased = int(earlier is not None)
    whole = lambda *shape: pl.BlockSpec(shape, lambda i: (0,) * len(shape))
    edge_spec = pl.BlockSpec((space, 2, GROUP, cols_n), lambda i: (0, 0, part // GROUP, 0))
    main_spec = pl.BlockSpec((space, 2, part, cols_n), lambda i: (0, 0, 0, 0))
    return pl.pallas_call(
        functools.partial(final_kernel, outer, chunk, aliased, part),
        grid=(1,),
        in_specs=[
            main_spec,
            main_spec,
            edge_spec,
            edge_spec,
            pl.BlockSpec((2, part, length), lambda i: (0, chunk, 0)),
            whole(2, GROUP, length),
            pl.BlockSpec((part, length), lambda i: (chunk, 0)),
            whole(outer, 2, 1, LANES),
            whole(2, 256, 256),
        ]
        + [pl.BlockSpec(memory_space=pl.ANY)] * aliased,
        out_specs=[
            pl.BlockSpec((2, 1, 2, part, length), lambda i: (0, 0, 0, chunk, 0)),
            whole(part, length),
        ],
        out_shape=[
            jax.ShapeDtypeStruct((2, 1, 2, part * chunks, length), jnp.float32),
            jax.ShapeDtypeStruct((part, length), jnp.float32),
        ],
        scratch_shapes=[
            pltpu.VMEM((outer, part + GROUP, 2 * LANES), jnp.float32),
            pltpu.VMEM((2, 2, part + 2 * GROUP, length), jnp.float32),
        ],
        input_output_aliases={9: 0} if aliased else {},
        compiler_params=pltpu.CompilerParams(vmem_limit_bytes=LIMIT),
        cost_estimate=pl.CostEstimate(
            flops=part * length * 15000, bytes_accessed=part * length * 60, transcendentals=0
        ),
    )(
        main[0],
        main[1],
        edge[0],
        edge[1],
        shift,
        shift_edge,
        beta,
        jnp.asarray(twiddles(outer, 0)),
        jnp.asarray(block_matrix(1.0, 1.0 / length, False)),
        *([earlier] if aliased else []),
    )


def wave_values(positions, length):
    outer = length // LANES
    natural_order = positions // LANES + outer * (positions % LANES)
    signed = jnp.where(natural_order < length // 2, natural_order, natural_order - length)
    return 2.0 * math.pi / length * signed.astype(jnp.float32)


def per_device(wavefields, frequencies, velocity, slab_owner, ref_velocity, ref_index):
    rows_n, width_y = wavefields.shape[3:]
    space = lax.axis_size("space")
    me = lax.axis_index("space")
    width_x = rows_n * space
    cols_n = width_y // space
    slab_local = velocity.shape[0]
    ref_count = ref_velocity.shape[1]
    chunks = 2 if rows_n >= 2 * LANES else 1
    part = rows_n // chunks
    omega = frequencies[0]

    owner = slab_owner[0]
    stored = lax.dynamic_index_in_dim(velocity, owner % slab_local, 0, keepdims=False)
    stored = jnp.where(lax.axis_index("freq") == owner // slab_local, stored, 0.0)
    first = forward_rows(wavefields, 0, space, cols_n)
    first, stored = lax.optimization_barrier((first, stored))
    speed = lax.psum(stored, "freq")

    swap = lambda x: lax.all_to_all(x, "space", split_axis=0, concat_axis=0, tiled=True)
    spectra = [swap(first), swap(forward_rows(wavefields, 1, space, cols_n))]
    spectra[1], speed = lax.optimization_barrier((spectra[1], speed))

    ky = wave_values(me * cols_n + jnp.arange(cols_n, dtype=jnp.int32), width_y)
    kx = wave_values(jnp.arange(width_x, dtype=jnp.int32), width_x)
    squared = kx[:, None] ** 2 + ky[None, :] ** 2
    vertical = (omega / ref_velocity[0][:, None, None]) ** 2 - squared[None]
    root = jnp.sqrt(jnp.abs(vertical))
    fits = vertical >= 0.0
    cosine = jnp.where(fits, jnp.cos(DZ * root), jnp.exp(-DZ * root))
    sine = jnp.where(fits, jnp.sin(DZ * root), 0.0)
    phase = jnp.stack([cosine, sine], axis=1).reshape(
        ref_count, 2, width_x // LANES, LANES, cols_n
    )

    count = space
    above = lax.ppermute(speed[-1:], "space", [(i, i + 1) for i in range(count - 1)])
    below = lax.ppermute(speed[:1], "space", [(i + 1, i) for i in range(count - 1)])
    edge_rows, edge_speed = [], []
    for h in range(chunks):
        for local, outside, kept in (
            (h * part - 1, h == 0, above),
            ((h + 1) * part, h == chunks - 1, below),
        ):
            edge_rows.append(local)
            edge_speed.append(kept if outside else speed[local : local + 1])
    while len(edge_rows) < GROUP:
        edge_rows.append(0)
        edge_speed.append(speed[:1])
    block_refs = ref_index[0]
    per_ref = width_x // block_refs.shape[0]

    def shifts(c, rows):
        inside = (rows >= 0) & (rows < width_x)
        cr = ref_velocity[0][block_refs[jnp.clip(rows, 0, width_x - 1) // per_ref]][:, None]
        safe = jnp.where(inside[:, None], c, 1.0)
        angle = omega * DZ * (1.0 / safe - 1.0 / cr)
        keep = inside[:, None].astype(jnp.float32)
        return jnp.stack([jnp.cos(angle) * keep, jnp.sin(angle) * keep]), cr

    start = me * rows_n
    shift, cr = shifts(speed, start + jnp.arange(rows_n, dtype=jnp.int32))
    beta = DZ * (speed - cr) * cr / (16.0 * omega)
    shift_edge, _ = shifts(
        jnp.concatenate(edge_speed, axis=0), start + jnp.array(edge_rows, dtype=jnp.int32)
    )

    moved = []
    for j in range(2):
        moved.append(middle(spectra[j], phase, block_refs, -1.0 if j == 0 else 1.0, chunks))
    back, latest = [], None
    for h in range(chunks):
        row = []
        for j in range(2):
            sent = moved[j][h]
            if h:
                sent, latest = lax.optimization_barrier((sent, latest))
                if j == 0:
                    back[-1][1] = latest
                else:
                    row[0] = latest
            latest = swap(sent)
            row.append(latest)
        back.append(row)
    fields, images = None, []
    for h in range(chunks):
        fields, image = final(back[h], back[0], shift, shift_edge, beta, h, chunks, fields)
        if h + 1 < chunks:
            images.append(jnp.sum(lax.all_gather(image, "freq"), axis=0))
        else:
            images.append(lax.psum(image, "freq"))
    return fields, jnp.concatenate(images, axis=0)[None]


def solution(mesh):
    in_specs = (
        P(None, "freq", None, "space", None),
        P("freq"),
        P("freq", "space", None),
        P(),
        P(),
        P(),
    )
    out_specs = (P(None, "freq", None, "space", None), P(None, "space", None))
    return jax.shard_map(
        per_device, mesh=mesh, in_specs=in_specs, out_specs=out_specs, check_vma=False
    )
```
